32 devices in a mesh: groups: 2 (over x), dp: 16 (over z, y, core).
Axes of the slice: x: 2, y: 2, z: 4, core: 2. Of those that a mesh axis runs over, the one named last changes fastest.
Arguments:
- image_embeds: bfloat16 [8192, 1280], P(('groups', 'dp')), parts along dimension 0, may hold values from -0.25 to 0.25
- text_embeds: bfloat16 [8192, 1280], P(('groups', 'dp')), parts along dimension 0, may hold values from -0.25 to 0.25
- labels: int32 [8192], P(('groups', 'dp')), parts along dimension 0, may hold values from 0 to 4095, as said below
Outputs:
- grad_images: float32 [8192, 1280], P(('groups', 'dp')), parts along dimension 0
- grad_texts: float32 [8192, 1280], P(('groups', 'dp')), parts along dimension 0
The draws below stay inside these ranges and needn't reach their ends.
There are 2 independent parts, one for each index of `groups`. The reference program is written for one: setup_inputs(seed, part) draws one part's arguments, and reference() takes and returns one part's arrays. A program takes and returns all parts, laid end to end along the dimension named above; each array names one. Nothing has to cross between parts.
Inputs may be any that keep to these rules, and one draw needn't show every extreme that they name: `labels`: each image row's matching text row lies in the same block of 256 rows, and each text row is the match of exactly one image row.
All inputs are finite; a program needn't handle non-finite values.
Results may differ from the reference program's by a relative error of at most 0.0025.
Values may be sent and summed in bfloat16 or wider, within the bound.
No kernel may reach another device: no remote copies, remote signals or barrier semaphores. Data moves between devices by JAX's collectives and lax.ppermute only.
A program may use at most 64 MiB of HBM per device.

```python
import math
import jax
import jax.numpy as jnp
from jax import lax

EMBED = 1280
ROWS = 256
WINDOW = 8
BATCH = 4096
N_DP = 16


def common(key):
    shared = jax.random.normal(jax.random.fold_in(key, 101), (BATCH, EMBED), jnp.float32) / math.sqrt(EMBED)
    perm_key = jax.random.fold_in(key, 102)
    block_count = BATCH // ROWS

    def one_block(block):
        return jax.random.permutation(jax.random.fold_in(perm_key, block), ROWS).astype(jnp.int32)
    perms = jax.vmap(one_block)(jnp.arange(block_count, dtype=jnp.int32))
    matching = (perms + jnp.arange(block_count, dtype=jnp.int32)[:, None] * ROWS).reshape(BATCH).astype(jnp.int32)
    return (shared, matching)


def row_scales(key, lowest, highest):
    return jnp.exp(jax.random.uniform(key, (BATCH, 1), jnp.float32, math.log(lowest), math.log(highest)))


def noise_normal(key):
    return jax.random.normal(key, (BATCH, EMBED), jnp.float32) / math.sqrt(EMBED)


def draw_image_embeds(key, part):
    shared, matching = common(key)
    key = jax.random.fold_in(key, 1)
    own_noise = noise_normal(jax.random.fold_in(key, 1))
    scales = row_scales(jax.random.fold_in(key, 2), 0.6, 1.6)
    embeds = scales * (math.sqrt(0.1) * shared + math.sqrt(0.4) * own_noise)
    return jnp.clip(embeds, -0.25, 0.25).astype(jnp.bfloat16)


def draw_text_embeds(key, part):
    shared, matching = common(key)
    key = jax.random.fold_in(key, 2)
    own_noise = noise_normal(jax.random.fold_in(key, 1))
    scales = row_scales(jax.random.fold_in(key, 2), 0.6, 1.6)
    by_image = scales * (math.sqrt(0.1) * shared + math.sqrt(0.4) * own_noise)
    embeds = jnp.zeros((BATCH, EMBED), jnp.float32).at[matching].set(by_image)
    return jnp.clip(embeds, -0.25, 0.25).astype(jnp.bfloat16)


def draw_labels(key, part):
    shared, matching = common(key)
    return matching


def setup_inputs(seed: int = 0, part: int = 0) -> dict:
    key_of = jax.random.split(jax.random.key(seed), 4)
    part_keys = jax.random.split(jax.random.fold_in(key_of[3], part), 4)
    image_embeds = draw_image_embeds(jax.random.fold_in(jax.random.fold_in(key_of[3], part), 71), part)
    text_embeds = draw_text_embeds(jax.random.fold_in(jax.random.fold_in(key_of[3], part), 71), part)
    labels = draw_labels(jax.random.fold_in(jax.random.fold_in(key_of[3], part), 71), part)
    return dict(image_embeds=image_embeds, text_embeds=text_embeds, labels=labels)


logit_scale = 100.0
half_scale = 50.0

def similarity(row_side, col_side):
    return logit_scale * jnp.dot(row_side, col_side.T, preferred_element_type=jnp.float32)

def weights(scores, row_norm, col_norm, positive):
    combined = jnp.exp(scores - row_norm[:, None]) + jnp.exp(scores - col_norm[None, :]) - 2.0 * positive.astype(jnp.float32)
    return combined.astype(jnp.bfloat16)

def window_ids(block, sign):
    steps = jnp.arange(WINDOW, dtype=jnp.int32)
    chosen = (block + sign * steps + N_DP) % N_DP
    return (chosen[:, None] * ROWS + jnp.arange(ROWS, dtype=jnp.int32)[None, :]).reshape(WINDOW * ROWS).astype(jnp.int32)

def reference(image_embeds, text_embeds, labels):
    blocks = jnp.arange(N_DP, dtype=jnp.int32)

    def row_block(block):
        own = lax.dynamic_slice_in_dim(image_embeds, block * ROWS, ROWS, 0)
        texts = jnp.take(text_embeds, window_ids(block, 1), axis=0)
        return jax.nn.logsumexp(similarity(own, texts), axis=1)

    def col_block(block):
        own = lax.dynamic_slice_in_dim(text_embeds, block * ROWS, ROWS, 0)
        images = jnp.take(image_embeds, window_ids(block, -1), axis=0)
        return jax.nn.logsumexp(similarity(images, own), axis=0)
    row_norm = lax.map(row_block, blocks).reshape(BATCH)
    col_norm = lax.map(col_block, blocks).reshape(BATCH)

    def image_grad(block):
        ids = window_ids(block, 1)
        own = lax.dynamic_slice_in_dim(image_embeds, block * ROWS, ROWS, 0)
        own_labels = lax.dynamic_slice_in_dim(labels, block * ROWS, ROWS, 0)
        own_norm = lax.dynamic_slice_in_dim(row_norm, block * ROWS, ROWS, 0)
        texts = jnp.take(text_embeds, ids, axis=0)
        cols = jnp.take(col_norm, ids, axis=0)
        mixing = weights(similarity(own, texts), own_norm, cols, own_labels[:, None] == ids[None, :])
        return half_scale * jnp.dot(mixing, texts, preferred_element_type=jnp.float32)

    def text_grad(block):
        ids = window_ids(block, -1)
        own = lax.dynamic_slice_in_dim(text_embeds, block * ROWS, ROWS, 0)
        own_norm = lax.dynamic_slice_in_dim(col_norm, block * ROWS, ROWS, 0)
        images = jnp.take(image_embeds, ids, axis=0)
        rows_norm = jnp.take(row_norm, ids, axis=0)
        far_labels = jnp.take(labels, ids, axis=0)
        targets = block * ROWS + jnp.arange(ROWS, dtype=jnp.int32)
        mixing = weights(similarity(images, own), rows_norm, own_norm, far_labels[:, None] == targets[None, :])
        return half_scale * jnp.dot(mixing.T, images, preferred_element_type=jnp.float32)
    grad_images = lax.map(image_grad, blocks).reshape(BATCH, EMBED)
    grad_texts = lax.map(text_grad, blocks).reshape(BATCH, EMBED)
    return (grad_images, grad_texts)
```

```python
import jax
import jax.numpy as jnp
from jax import lax
from jax.sharding import PartitionSpec as P

WINDOW = 8
LEVEL = 4


logit_scale = 100.0
half_scale = 50.0


def route(count, moves):
    return [
        ((level * LEVEL + a) % count, (level * LEVEL + b) % count)
        for level in range(count // LEVEL)
        for a, b in moves
    ]


def exchange(text, image, rank):
    count = lax.axis_size("dp")

    def send(block, moves):
        return lax.ppermute(block, "dp", route(count, moves))

    low_y = rank < 2
    even = rank % 2 == 0
    cores = [(0, 1), (1, 0), (2, 3), (3, 2)]
    across = [(0, 2), (1, 3), (2, 0), (3, 1)]
    t1 = send(text, [(r + 4, r) for r in range(4)])
    own_y = send(jnp.where(low_y, image, text), across)
    own_c = send(jnp.where(even, image, text), cores)
    i1 = send(image, [(r - 4, r) for r in range(4)])
    t2 = send(t1, [(r + 4, r) for r in (0, 1, 2)])
    i2 = send(i1, [(r - 4, r) for r in (1, 2, 3)])
    own_yc = send(own_y, cores)
    t1_c = send(t1, cores)
    t1_y = send(t1, across)
    i1_c = send(i1, cores)
    i1_y = send(i1, across)
    t1_yc = send(t1_y, cores)
    i1_yc = send(i1_y, cores)
    two_c = send(jnp.where(even, t2, i2), cores)
    two_y = send(jnp.where(low_y, t2, i2), across)
    two_yc = send(two_y, cores)
    texts = [
        text, t1, t1_c, t1_y, t1_yc,
        jnp.where(even, own_c, two_c),
        jnp.where(low_y, own_y, two_y),
        jnp.where(low_y, own_yc, two_yc),
    ]
    images = [
        image, i1, i1_c, i1_y, i1_yc,
        jnp.where(even, two_c, own_c),
        jnp.where(low_y, two_y, own_y),
        jnp.where(low_y, two_yc, own_yc),
    ]
    return texts, images


TEXT_PLACES = (
    (0, 4, 5, 6, 7, 1, 2, 3),
    (1, 5, 4, 7, 6, 8, 3, 2),
    (2, 6, 7, 4, 5, 3, 8, 9),
    (3, 7, 6, 5, 4, 10, 9, 8),
)
IMAGE_PLACES = tuple(tuple(3 - place for place in row) for row in TEXT_PLACES[::-1])


def similarity(row_side, col_side):
    products = lax.dot_general(
        row_side, col_side, (((1,), (1,)), ((), ())), preferred_element_type=jnp.float32
    )
    return logit_scale * products


def log_sums(blocks, reduce_dim):
    peak = jnp.max(jnp.stack([jnp.max(b, axis=reduce_dim) for b in blocks]), axis=0)
    total = sum(
        jnp.sum(jnp.exp(b - jnp.expand_dims(peak, reduce_dim)), axis=reduce_dim) for b in blocks
    )
    return peak + jnp.log(total)


def weights(scores, row_norm, col_norm, positive=None):
    combined = jnp.exp(scores - row_norm[:, None]) + jnp.exp(scores - col_norm[None, :])
    if positive is not None:
        combined = combined - 2.0 * positive.astype(jnp.float32)
    return combined.astype(jnp.bfloat16)


def shards(image_embeds, text_embeds, labels):
    row_count = image_embeds.shape[0]
    count = lax.axis_size("dp")
    here = lax.axis_index("dp")
    rank = here % LEVEL
    positions = here * row_count + jnp.arange(row_count, dtype=jnp.int32)
    texts, images = exchange(text_embeds, image_embeds, rank)
    row_scores = [similarity(image_embeds, t) for t in texts]
    col_scores = [similarity(i, text_embeds) for i in images]
    row_norm = log_sums(row_scores, 1)
    col_norm = log_sums(col_scores, 0)
    norms = jnp.stack([row_norm, col_norm])
    table = lax.all_to_all(
        jnp.broadcast_to(norms[None], (count, *norms.shape)), "dp", 0, 0, tiled=False
    )
    level = here - rank
    text_at = (level + jnp.array(TEXT_PLACES, jnp.int32)[rank] + count) % count
    image_at = (level + jnp.array(IMAGE_PLACES, jnp.int32)[rank] + count) % count
    positive = labels[:, None] == positions[None, :]
    image_sum = 0.0
    text_sum = 0.0
    for slot in range(WINDOW):
        own = positive if slot == 0 else None
        far_cols = lax.dynamic_index_in_dim(table, text_at[slot], 0, False)[1]
        mixing = weights(row_scores[slot], row_norm, far_cols, own)
        image_sum += jnp.dot(mixing, texts[slot], preferred_element_type=jnp.float32)
        far_rows = lax.dynamic_index_in_dim(table, image_at[slot], 0, False)[0]
        mixing = weights(col_scores[slot], far_rows, col_norm, own)
        text_sum += lax.dot_general(
            mixing, images[slot], (((0,), (0,)), ((), ())), preferred_element_type=jnp.float32
        )
    return (half_scale * image_sum, half_scale * text_sum)


def solution(mesh):
    return jax.shard_map(
        shards,
        mesh=mesh,
        in_specs=(P(("groups", "dp"), None), P(("groups", "dp"), None), P(("groups", "dp"))),
        out_specs=(P(("groups", "dp"), None), P(("groups", "dp"), None)),
        check_vma=False,
    )
```

```python
import jax
import jax.numpy as jnp
from jax import lax
from jax.experimental import pallas as pl
from jax.experimental.pallas import tpu as pltpu
from jax.sharding import PartitionSpec as P

WINDOW = 8
LEVEL = 4
ROW_PLACE = 16
TABLE_ROWS = 24

logit_scale = 100.0
half_scale = 50.0
vmem_bytes = 48 * 1024 * 1024


def send(block, moves):
    count = lax.axis_size("dp")
    route = [
        ((level * LEVEL + a) % count, (level * LEVEL + b) % count)
        for level in range(count // LEVEL)
        for a, b in moves
    ]
    return lax.ppermute(block, "dp", route)


def after(block, *earlier):
    return lax.optimization_barrier((block, *earlier))[0]


def scores_of(rows, cols):
    products = lax.dot_general(
        rows, cols, (((1,), (1,)), ((), ())), preferred_element_type=jnp.float32
    )
    return logit_scale * products


def as_column(row):
    return jnp.transpose(jnp.broadcast_to(row, (128, row.shape[1])))[:, :1]


def as_row(column):
    return jnp.transpose(jnp.broadcast_to(column, (column.shape[0], 128)))[:1, :]


def near_offsets(rank):
    return 0, 4, 5 - 2 * (rank % 2), 6 - 4 * (rank // 2), 7 - 2 * rank


def for_far(rank, pairs, body):
    even = rank % 2 == 0
    low = rank < 2
    cases = (
        (even, pairs[0], 1),
        (jnp.logical_not(even), pairs[1], 7),
        (low, pairs[2], 2),
        (jnp.logical_not(low), pairs[3], 6),
        (low, pairs[4], 3 - 2 * rank),
        (jnp.logical_not(low), pairs[5], 11 - 2 * rank),
    )
    for index, (chosen, ref, offset) in enumerate(cases):
        pl.when(chosen)(lambda: body(index // 2, ref, offset))


def near_scores(*refs):
    own, others = refs[0], refs[1:6]
    score_ref, peak_ref, total_ref, stat_ref = refs[6:]
    rank = lax.axis_index("dp") % LEVEL
    offsets = near_offsets(rank)
    stat_ref[...] = jnp.zeros_like(stat_ref)
    for slot, other in enumerate(others):
        scores = scores_of(own[...], other[...])
        score_ref[slot] = scores
        peak = jnp.max(scores, axis=0, keepdims=True)
        total = jnp.sum(jnp.exp(scores - peak), axis=0, keepdims=True)
        stat_ref[pl.ds(offsets[slot], 1), :] = peak
        stat_ref[pl.ds(WINDOW + offsets[slot], 1), :] = total
    peak = jnp.max(jnp.max(score_ref[...], axis=0), axis=1, keepdims=True)
    shifted = jnp.exp(score_ref[...] - peak[None])
    total = jnp.sum(jnp.sum(shifted, axis=0), axis=1, keepdims=True)
    peak_ref[...] = jnp.broadcast_to(peak, peak_ref.shape)
    total_ref[...] = jnp.broadcast_to(total, total_ref.shape)


def far_scores(*refs):
    own, pairs = refs[0], refs[1:7]
    near_peak, near_total, near_stat = refs[7:10]
    score_ref, norm_ref, table_ref, stat_ref = refs[10:]
    rank = lax.axis_index("dp") % LEVEL
    stat_ref[...] = near_stat[...]

    def one(slot, other, offset):
        scores = scores_of(own[...], other[...])
        score_ref[slot] = scores
        peak = jnp.max(scores, axis=0, keepdims=True)
        total = jnp.sum(jnp.exp(scores - peak), axis=0, keepdims=True)
        stat_ref[pl.ds(offset, 1), :] = peak
        stat_ref[pl.ds(WINDOW + offset, 1), :] = total

    for_far(rank, pairs, one)
    old_peak = near_peak[:, :1]
    peak = jnp.max(jnp.max(score_ref[...], axis=0), axis=1, keepdims=True)
    peak = jnp.maximum(peak, old_peak)
    shifted = jnp.exp(score_ref[...] - peak[None])
    total = jnp.sum(jnp.sum(shifted, axis=0), axis=1, keepdims=True)
    total = total + near_total[:, :1] * jnp.exp(old_peak - peak)
    norm = peak + jnp.log(total)
    norm_ref[...] = jnp.broadcast_to(norm, norm_ref.shape)
    stat_ref[pl.ds(ROW_PLACE, 1), :] = as_row(norm)
    for index in range(table_ref.shape[0]):
        table_ref[index] = stat_ref[...]


def merged_column(table, text):
    count = table.shape[0]
    peaks = []
    totals = []
    for offset in range(WINDOW):
        source = (text - offset + count) % count
        peaks.append(table[source, pl.ds(offset, 1), :])
        totals.append(table[source, pl.ds(WINDOW + offset, 1), :])
    peaks = jnp.concatenate(peaks, axis=0)
    totals = jnp.concatenate(totals, axis=0)
    peak = jnp.max(peaks, axis=0, keepdims=True)
    total = jnp.sum(totals * jnp.exp(peaks - peak), axis=0, keepdims=True)
    return peak + jnp.log(total)


def mixed(scores, self_norm, other_norm, positive=None):
    combined = jnp.exp(scores - self_norm) + jnp.exp(scores - other_norm)
    if positive is not None:
        combined = combined - 2.0 * positive.astype(jnp.float32)
    return combined.astype(jnp.bfloat16)


def image_products(*refs):
    label_ref, norm_ref, table, near_ref, far_ref = refs[:5]
    near, pairs = refs[5:10], refs[10:16]
    out_ref = refs[16]
    here = lax.axis_index("dp")
    rank = here % LEVEL
    count = table.shape[0]
    norm = norm_ref[:, :1]
    rows = out_ref.shape[0]
    offsets = near_offsets(rank)
    for slot, other in enumerate(near):
        positive = None
        if slot == 0:
            lane = lax.broadcasted_iota(jnp.int32, (rows, rows), 1)
            positive = label_ref[...] == here * rows + lane
        col = merged_column(table, (here + offsets[slot]) % count)
        mixing = mixed(near_ref[slot], norm, col, positive)
        product = jnp.dot(mixing, other[...], preferred_element_type=jnp.float32)
        if slot == 0:
            out_ref[...] = product
        else:
            out_ref[...] += product

    def one(slot, other, offset):
        col = merged_column(table, (here + offset) % count)
        mixing = mixed(far_ref[slot], norm, col)
        out_ref[...] += jnp.dot(mixing, other[...], preferred_element_type=jnp.float32)

    for_far(rank, pairs, one)
    out_ref[...] = half_scale * out_ref[...]


def near_text_products(*refs):
    label_ref, table, own = refs[:3]
    near = refs[3:8]
    out_ref, norm_ref = refs[8:]
    here = lax.axis_index("dp")
    rank = LEVEL - 1 - here % LEVEL
    count = table.shape[0]
    rows = out_ref.shape[0]
    norm = as_column(merged_column(table, here))
    norm_ref[...] = jnp.broadcast_to(norm, norm_ref.shape)
    offsets = near_offsets(rank)
    for slot, other in enumerate(near):
        positive = None
        if slot == 0:
            sublane = lax.broadcasted_iota(jnp.int32, (rows, rows), 0)
            positive = label_ref[...] == here * rows + sublane
        source = (here - offsets[slot] + count) % count
        row = table[source, pl.ds(ROW_PLACE, 1), :]
        mixing = mixed(scores_of(own[...], other[...]), norm, row, positive)
        product = jnp.dot(mixing, other[...], preferred_element_type=jnp.float32)
        if slot == 0:
            out_ref[...] = product
        else:
            out_ref[...] += product


def far_text_products(*refs):
    norm_ref, table, own, sum_ref = refs[:4]
    pairs = refs[4:10]
    out_ref = refs[10]
    here = lax.axis_index("dp")
    rank = LEVEL - 1 - here % LEVEL
    count = table.shape[0]
    norm = norm_ref[:, :1]
    out_ref[...] = sum_ref[...]

    def one(slot, other, offset):
        source = (here - offset + count) % count
        row = table[source, pl.ds(ROW_PLACE, 1), :]
        mixing = mixed(scores_of(own[...], other[...]), norm, row)
        out_ref[...] += jnp.dot(mixing, other[...], preferred_element_type=jnp.float32)

    for_far(rank, pairs, one)
    out_ref[...] = half_scale * out_ref[...]


def kernel_call(body, outs, blocks, *operands):
    flops = 2 * 256 * 256 * 1280 * blocks
    return pl.pallas_call(
        body,
        out_shape=outs,
        in_specs=[pl.BlockSpec(memory_space=pltpu.VMEM)] * len(operands),
        out_specs=[pl.BlockSpec(memory_space=pltpu.VMEM)] * len(outs),
        compiler_params=pltpu.CompilerParams(vmem_limit_bytes=vmem_bytes),
        cost_estimate=pl.CostEstimate(
            flops=flops, bytes_accessed=blocks * 800000, transcendentals=blocks * 65536 * 2
        ),
        name=body.__name__,
    )(*operands)


cores = [(0, 1), (1, 0), (2, 3), (3, 2)]
across = [(0, 2), (1, 3), (2, 0), (3, 1)]


def shards(image, text, labels):
    rows, width = image.shape
    count = lax.axis_size("dp")
    f32 = jnp.float32

    t1 = send(text, [(r + 4, r) for r in range(4)])
    own_y_t = send(text, [(2, 0), (3, 1)])
    own_y_i = send(image, [(0, 2), (1, 3)])
    own_c_t = send(text, [(1, 0), (3, 2)])
    own_c_i = send(image, [(0, 1), (2, 3)])
    t2 = send(t1, [(r + 4, r) for r in (0, 1, 2)])
    t1_y = send(after(t1, own_y_t, own_y_i), across)
    t1_c = send(t1, cores)
    own_yc_t = send(own_y_t, [(0, 1), (1, 0)])
    own_yc_i = send(own_y_i, [(2, 3), (3, 2)])
    t1_yc = send(t1_y, cores)
    t2_y = send(after(t2, t1_y), [(0, 2), (1, 3)])
    t2_c = send(t2, [(0, 1), (2, 3)])
    t2_yc = send(t2_y, [(2, 3), (3, 2)])

    i1 = send(after(image, t1), [(r - 4, r) for r in range(4)])
    i2 = send(i1, [(r - 4, r) for r in (1, 2, 3)])
    i1_c = send(i1, cores)
    i1_y = send(after(i1, t1_y), across)
    i1_yc = send(i1_y, cores)
    i2_y = send(after(i2, i1_y), [(2, 0), (3, 1)])
    i2_c = send(i2, [(3, 2), (1, 0)])
    i2_yc = send(i2_y, [(0, 1), (1, 0)])

    near_t = [text, t1, t1_c, t1_y, t1_yc]
    far_t = [own_c_t, t2_c, own_y_t, t2_y, own_yc_t, t2_yc]
    near_i = [image, i1, i1_c, i1_y, i1_yc]
    far_i = [own_c_i, i2_c, own_y_i, i2_y, own_yc_i, i2_yc]

    def struct(*shape):
        return jax.ShapeDtypeStruct(shape, f32)

    near_s, peak, total, stat = kernel_call(
        near_scores,
        [struct(5, rows, rows), struct(rows, 128), struct(rows, 128), struct(TABLE_ROWS, rows)],
        5, image, *near_t,
    )
    far_s, norm, message, _ = kernel_call(
        far_scores,
        [struct(3, rows, rows), struct(rows, 128), struct(count, TABLE_ROWS, rows),
         struct(TABLE_ROWS, rows)],
        3, image, *far_t, peak, total, stat,
    )
    table = lax.all_to_all(message, "dp", 0, 0, tiled=True)
    (grad_images,) = kernel_call(
        image_products, [struct(rows, width)], 8,
        labels[:, None], norm, table, near_s, far_s, *near_t, *far_t,
    )
    near_sum, col_norm = kernel_call(
        near_text_products, [struct(rows, width), struct(rows, 128)], 10,
        labels[None, :], table, text, *near_i,
    )
    (grad_texts,) = kernel_call(
        far_text_products, [struct(rows, width)], 6, col_norm, table, text, near_sum, *far_i,
    )
    return grad_images, grad_texts


def solution(mesh):
    return jax.shard_map(
        shards,
        mesh=mesh,
        in_specs=(P(("groups", "dp"), None), P(("groups", "dp"), None), P(("groups", "dp"))),
        out_specs=(P(("groups", "dp"), None), P(("groups", "dp"), None)),
        check_vma=False,
    )
```

```python
import jax
import jax.numpy as jnp
from jax import lax
from jax.experimental import pallas as pl
from jax.experimental.pallas import tpu as pltpu
from jax.sharding import PartitionSpec as P

WINDOW = 8
LEVEL = 4
ROW_PLACE = 16
TABLE_ROWS = 24

logit_scale = 100.0
half_scale = 50.0
vmem_bytes = 60 * 1024 * 1024


def send(block, moves):
    count = lax.axis_size("dp")
    route = [
        ((level * LEVEL + a) % count, (level * LEVEL + b) % count)
        for level in range(count // LEVEL)
        for a, b in moves
    ]
    return lax.ppermute(block, "dp", route)


def after(block, *earlier):
    return lax.optimization_barrier((block, *earlier))[0]


def scores_of(rows, cols):
    products = lax.dot_general(
        rows, cols, (((1,), (1,)), ((), ())), preferred_element_type=jnp.float32
    )
    return logit_scale * products


def as_column(row):
    return jnp.transpose(jnp.broadcast_to(row, (128, row.shape[1])))[:, :1]


def as_row(column):
    return jnp.transpose(jnp.broadcast_to(column, (column.shape[0], 128)))[:1, :]


class Loads:
    def __init__(self, sems):
        self.sems = sems
        self.used = 0

    def slot(self, ref):
        self.used += 1
        return ref, self.sems.at[self.used - 1]

    def load(self, dest, *cases):
        slot = self.slot(dest)
        for chosen, ref in cases:
            if chosen is None:
                pltpu.make_async_copy(ref, *slot).start()
            else:
                pl.when(chosen)(pltpu.make_async_copy(ref, *slot).start)
        return slot

    def store(self, source, dest):
        copy = pltpu.make_async_copy(source, *self.slot(dest))
        copy.start()
        return copy


def arrived(*slots):
    for ref, sem in slots:
        pltpu.make_async_copy(ref, ref, sem).wait()


def part(ref, slot, rows):
    return ref.at[pl.ds(slot * rows, rows)]


def place():
    here = lax.axis_index("dp")
    rank = here % LEVEL
    return here, rank // 2, rank % 2


def put_stats(scores, stat_ref, offset):
    peak = jnp.max(scores, axis=0, keepdims=True)
    total = jnp.sum(jnp.exp(scores - peak), axis=0, keepdims=True)
    stat_ref[pl.ds(offset, 1), :] = peak
    stat_ref[pl.ds(WINDOW + offset, 1), :] = total


def row_stats(scores):
    peak = jnp.max(jnp.max(scores, axis=0), axis=1, keepdims=True)
    total = jnp.sum(jnp.sum(jnp.exp(scores - peak[None]), axis=0), axis=1, keepdims=True)
    return peak, total


def merge(peak_a, total_a, peak_b, total_b):
    peak = jnp.maximum(peak_a, peak_b)
    return peak, total_a * jnp.exp(peak_a - peak) + total_b * jnp.exp(peak_b - peak)


def near_scores(image, sibling, text, t1, t1_y, *refs):
    rows_ref, stat_ref, held, own_ref, sib_ref, sems = refs
    rows = image.shape[0]
    _, q, c = place()
    loads = Loads(sems)
    blocks = [part(held, slot, rows) for slot in range(5)]
    arrived(
        *[
            loads.load(block, (None, ref))
            for block, ref in zip(blocks, (image, sibling, text, t1, t1_y))
        ]
    )
    own, sib, *texts = blocks
    offsets = (0, 4, 6 - 4 * q)
    sib_offsets = (3 + 2 * c, 5 - 4 * q + 2 * c)
    stat_ref[...] = jnp.zeros_like(stat_ref)
    for slot, block in enumerate(texts):
        own_ref[slot] = scores_of(own[...], block[...])
        if slot > 0:
            sib_ref[slot - 1] = scores_of(sib[...], block[...])
    for slot in range(3):
        put_stats(own_ref[slot], stat_ref, offsets[slot])
    for slot in range(2):
        put_stats(sib_ref[slot], stat_ref, sib_offsets[slot])
    lane = lax.broadcasted_iota(jnp.int32, rows_ref.shape, 1)
    columns = (*row_stats(own_ref[...]), *row_stats(sib_ref[...]))
    packed = jnp.zeros(rows_ref.shape, jnp.float32)
    for index, column in enumerate(columns):
        packed = jnp.where(lane == index, column, packed)
    rows_ref[...] = packed


def far_scores(near_rows, near_stat, image, sibling, text, t2_lo, t2_hi, own_y, t2_y, *refs):
    message_ref, held, own_ref, sib_ref, stat_ref, sems = refs
    rows = image.shape[0]
    _, q, c = place()
    loads = Loads(sems)
    own, sib, block, last = [part(held, slot, rows) for slot in range(4)]
    arrived(
        loads.load(own, (None, image)),
        loads.load(block, (q == 0, own_y), (q == 1, t2_y)),
        loads.load(sib, (None, sibling)),
        loads.load(last, *last_cases(q, c == 0, t2_lo, t2_hi, text)),
    )
    stat_ref[...] = near_stat[...]
    offset = 2 + 4 * q
    own_ref[0] = scores_of(own[...], block[...])
    sib_ref[0] = scores_of(sib[...], block[...])
    sib_ref[1] = scores_of(sib[...], last[...])
    put_stats(own_ref[0], stat_ref, offset)
    put_stats(sib_ref[0], stat_ref, offset + 2 * c - 1)
    put_stats(sib_ref[1], stat_ref, 7 - 6 * c)
    columns = [near_rows[:, index:index + 1] for index in range(4)]
    own_rows = merge(*columns[:2], *row_stats(own_ref[...]))
    sib_rows = merge(*columns[2:], *row_stats(sib_ref[...]))
    for index, column in enumerate((*own_rows, *sib_rows)):
        stat_ref[pl.ds(ROW_PLACE + index, 1), :] = as_row(column)
    for index in range(message_ref.shape[0]):
        message_ref[index] = stat_ref[...]


def last_cases(q, moved, low_block, high_block, own):
    return (
        (jnp.logical_and(moved, q == 0), low_block),
        (jnp.logical_and(moved, q == 1), high_block),
        (jnp.logical_not(moved), own),
    )


def sibling_of(index):
    return index + 1 - 2 * (index % 2)


def column_norm(table, text):
    count = table.shape[0]
    text = text % count
    peaks = []
    totals = []
    for offset in range(WINDOW):
        source = (text - offset + count) % count
        if offset % 2:
            source = sibling_of(source)
        peaks.append(table[source, pl.ds(offset, 1), :])
        totals.append(table[source, pl.ds(WINDOW + offset, 1), :])
    peaks = jnp.concatenate(peaks, axis=0)
    totals = jnp.concatenate(totals, axis=0)
    peak = jnp.max(peaks, axis=0, keepdims=True)
    total = jnp.sum(totals * jnp.exp(peaks - peak), axis=0, keepdims=True)
    return peak + jnp.log(total)


def row_norms(table, images):
    count = table.shape[0]
    images = [(image + count) % count for image in images]

    def rows_of(sources, place):
        return jnp.concatenate([table[s, pl.ds(place, 1), :] for s in sources], axis=0)

    others = [sibling_of(image) for image in images]
    peak, total = merge(
        rows_of(images, ROW_PLACE),
        rows_of(images, ROW_PLACE + 1),
        rows_of(others, ROW_PLACE + 2),
        rows_of(others, ROW_PLACE + 3),
    )
    return peak + jnp.log(total)


def mixed(scores, self_norm, other_norm, positive=None):
    combined = jnp.exp(scores - self_norm) + jnp.exp(scores - other_norm)
    if positive is not None:
        combined = combined - 2.0 * positive.astype(jnp.float32)
    return combined.astype(jnp.bfloat16)


def wide_products(loads, mixing, blocks, out_ref, out):
    width = blocks.shape[1]
    step = 256 if width % 256 == 0 else width
    stores = []
    for start in range(0, width, step):
        cols = slice(start, start + step)
        product = jnp.dot(mixing[...], blocks[:, cols], preferred_element_type=jnp.float32)
        out_ref[:, cols] = half_scale * product
        stores.append(loads.store(out_ref.at[:, cols], out.at[:, cols]))
    return stores


def tile_products(loads, own, sib, blocks, norms, others, positive, mixes, out_refs, outs):
    rows = own.shape[0]
    for slot in range(4):
        block = part(blocks, slot, rows)
        mixes[0][:, slot * rows:(slot + 1) * rows] = mixed(
            scores_of(own[...], block[...]), norms[0], others[slot],
            positive if slot == 0 else None,
        )
    stores = wide_products(
        loads, mixes[0], blocks.at[pl.ds(0, 4 * rows)], out_refs[0], outs[0]
    )
    for slot in range(1, 5):
        block = part(blocks, slot, rows)
        mixes[1][:, (slot - 1) * rows:slot * rows] = mixed(
            scores_of(sib[...], block[...]), norms[1], others[slot]
        )
    stores += wide_products(
        loads, mixes[1], blocks.at[pl.ds(rows, 4 * rows)], out_refs[1], outs[1]
    )
    for store in stores:
        store.wait()


def image_products(label_ref, table_in, image, sibling, *refs):
    text, t1, t1_y, t2_lo, t2_hi, own_y, t2_y = refs[:7]
    outs, (held, blocks, table, *more) = refs[7:9], refs[9:]
    mixes, out_refs, sems = more[:2], more[2:4], more[4]
    rows = image.shape[0]
    here, q, c = place()
    loads = Loads(sems)
    own, sib = part(held, 0, rows), part(held, 1, rows)
    cases = (
        ((None, text),),
        ((None, t1),),
        ((None, t1_y),),
        ((q == 0, own_y), (q == 1, t2_y)),
        last_cases(q, c == 0, t2_lo, t2_hi, text),
    )
    arrived(
        loads.load(table, (None, table_in)),
        loads.load(own, (None, image)),
        loads.load(sib, (None, sibling)),
        *[loads.load(part(blocks, slot, rows), *case) for slot, case in enumerate(cases)],
    )
    sib_place = sibling_of(here)
    norms = row_norms(table, [here, sib_place])
    norms = [as_column(norms[:1]), as_column(norms[1:])]
    offsets = (0, 4, 6 - 4 * q, 2 + 4 * q, 8 - 8 * c)
    others = [column_norm(table, here + offset) for offset in offsets]
    lane = lax.broadcasted_iota(jnp.int32, (rows, rows), 1)
    match = as_column(label_ref[...].astype(jnp.float32)).astype(jnp.int32)
    positive = match == here * rows + lane
    tile_products(loads, own, sib, blocks, norms, others, positive, mixes, out_refs, outs)


def text_products(label_ref, table_in, text, sibling, *refs):
    image, i1_lo, i1_hi, i1_up, i1_down, i2_lo, i2_hi, own_y, i2_y = refs[:9]
    outs, (held, blocks, table, *more) = refs[9:11], refs[11:]
    mixes, out_refs, sems = more[:2], more[2:4], more[4]
    rows = text.shape[0]
    here, q, c = place()
    loads = Loads(sems)
    own, sib = part(held, 0, rows), part(held, 1, rows)
    cases = (
        ((None, image),),
        ((q == 0, i1_lo), (q == 1, i1_hi)),
        ((q == 0, i1_up), (q == 1, i1_down)),
        ((q == 0, i2_y), (q == 1, own_y)),
        last_cases(q, c == 1, i2_lo, i2_hi, image),
    )
    arrived(
        loads.load(table, (None, table_in)),
        loads.load(own, (None, text)),
        loads.load(sib, (None, sibling)),
        *[loads.load(part(blocks, slot, rows), *case) for slot, case in enumerate(cases)],
    )
    norms = [as_column(column_norm(table, index)) for index in (here, sibling_of(here))]
    offsets = (0, 4, 2 + 4 * q, 6 - 4 * q, 8 * c)
    others = row_norms(table, [here - offset for offset in offsets])
    others = [others[slot:slot + 1] for slot in range(5)]
    sublane = lax.broadcasted_iota(jnp.int32, (rows, rows), 0)
    positive = label_ref[...] == here * rows + sublane
    tile_products(loads, own, sib, blocks, norms, others, positive, mixes, out_refs, outs)


def kernel_call(body, outs, scratch, copies, whole, blocks):
    spaces = [pltpu.VMEM] * len(whole) + [pl.ANY] * len(blocks)
    return pl.pallas_call(
        body,
        out_shape=[out for _, out in outs],
        in_specs=[pl.BlockSpec(memory_space=space) for space in spaces],
        out_specs=[pl.BlockSpec(memory_space=space) for space, _ in outs],
        scratch_shapes=[*scratch, pltpu.SemaphoreType.DMA((copies,))],
        compiler_params=pltpu.CompilerParams(vmem_limit_bytes=vmem_bytes),
        cost_estimate=pl.CostEstimate(
            flops=1000000, bytes_accessed=100000, transcendentals=1000
        ),
        name=body.__name__,
    )(*whole, *blocks)


cores = [(0, 1), (1, 0), (2, 3), (3, 2)]
across = [(0, 2), (1, 3), (2, 0), (3, 1)]


def shards(image, text, labels):
    rows, width = image.shape
    count = lax.axis_size("dp")
    f32 = jnp.float32

    def struct(*shape):
        return jax.ShapeDtypeStruct(shape, f32)

    def square(blocks):
        return pltpu.VMEM((blocks, rows, rows), f32)

    def wide(blocks, dtype=jnp.bfloat16):
        return pltpu.VMEM((blocks * rows, width), dtype)

    t1 = send(text, [(r + 4, r) for r in range(4)])
    own_y_t = send(text, [(2, 0), (3, 1)])
    own_y_i = send(image, [(0, 2), (1, 3)])
    image_c = send(image, cores)
    text_c = send(text, cores)
    t2_lo = send(t1, [(4, 0), (5, 1)])
    t2_hi = send(t1, [(6, 2)])
    t1_y = send(after(t1, own_y_t, own_y_i, image_c), across)
    i1_hi = send(after(image, t1), [(-2, 2), (-1, 3)])
    t2_y = send(after(t2_lo, t1_y), [(0, 2), (1, 3)])
    i1_lo = send(after(image, t2_lo), [(-4, 0), (-3, 1)])
    near_rows, near_stat = kernel_call(
        near_scores,
        [(pltpu.VMEM, struct(rows, 128)), (pltpu.VMEM, struct(TABLE_ROWS, rows))],
        [wide(5), square(3), square(2)], 5, [], [image, image_c, text, t1, t1_y],
    )
    i1_up = send(i1_hi, [(2, 0), (3, 1)])
    i2_hi = send(i1_hi, [(-2, 2), (-1, 3)])
    near_rows = after(near_rows, i1_lo, i1_up)
    (message,) = kernel_call(
        far_scores, [(pltpu.VMEM, struct(count, TABLE_ROWS, rows))],
        [wide(4), square(1), square(2), pltpu.VMEM((TABLE_ROWS, rows), f32)], 4,
        [near_rows, near_stat], [image, image_c, text, t2_lo, t2_hi, own_y_t, t2_y],
    )
    i1_down = send(i1_lo, [(0, 2), (1, 3)])
    i2_lo = send(i1_lo, [(-3, 1)])
    i2_y = send(i2_hi, [(2, 0), (3, 1)])
    table = lax.all_to_all(after(message, i2_lo, i2_hi), "dp", 0, 0, tiled=True)

    def tile_call(body, whole, blocks):
        mix = pltpu.VMEM((rows, 4 * rows), jnp.bfloat16)
        return kernel_call(
            body, [(pl.ANY, struct(rows, width))] * 2,
            [wide(2), wide(5), pltpu.VMEM((count, TABLE_ROWS, rows), f32), mix, mix,
             wide(1, f32), wide(1, f32)], 24, whole, blocks,
        )

    label_row = labels[None, :]
    own_image, sib_image = tile_call(
        image_products, [label_row],
        [table, image, image_c, text, t1, t1_y, t2_lo, t2_hi, own_y_t, t2_y],
    )
    table = after(table, own_image)
    own_text, sib_text = tile_call(
        text_products, [label_row],
        [table, text, text_c, image, i1_lo, i1_hi, i1_up, i1_down, i2_lo, i2_hi, own_y_i, i2_y],
    )
    return own_image + send(sib_image, cores), own_text + send(sib_text, cores)


def solution(mesh):
    return jax.shard_map(
        shards,
        mesh=mesh,
        in_specs=(P(("groups", "dp"), None), P(("groups", "dp"), None), P(("groups", "dp"))),
        out_specs=(P(("groups", "dp"), None), P(("groups", "dp"), None)),
        check_vma=False,
    )
```

```python
import jax
import jax.numpy as jnp
from jax import lax
from jax.experimental import pallas as pl
from jax.experimental.pallas import tpu as pltpu
from jax.sharding import PartitionSpec as P

WINDOW = 8
LEVEL = 4
ROW_PLACE = 16
TABLE_ROWS = 24

logit_scale = 100.0
half_scale = 50.0
vmem_bytes = 60 * 1024 * 1024


def send(block, moves):
    count = lax.axis_size("dp")
    route = [
        ((level * LEVEL + a) % count, (level * LEVEL + b) % count)
        for level in range(count // LEVEL)
        for a, b in moves
    ]
    return lax.ppermute(block, "dp", route)


def after(block, *earlier):
    return lax.optimization_barrier((block, *earlier))[0]


def scores_of(rows, cols):
    products = lax.dot_general(
        rows, cols, (((1,), (1,)), ((), ())), preferred_element_type=jnp.float32
    )
    return logit_scale * products


def as_column(row):
    return jnp.transpose(jnp.broadcast_to(row, (128, row.shape[1])))[:, :1]


def as_row(column):
    return jnp.transpose(jnp.broadcast_to(column, (column.shape[0], 128)))[:1, :]


class Loads:
    def __init__(self, sems):
        self.sems = sems
        self.used = 0

    def slot(self, ref):
        self.used += 1
        return ref, self.sems.at[self.used - 1]

    def load(self, dest, *cases):
        slot = self.slot(dest)
        for chosen, ref in cases:
            copy = pltpu.make_async_copy(ref, *slot)
            if chosen is None:
                copy.start()
            else:
                pl.when(chosen)(copy.start)
        return slot

    def store(self, source, dest):
        copy = pltpu.make_async_copy(source, *self.slot(dest))
        copy.start()
        return copy


def arrived(*slots):
    for ref, sem in slots:
        pltpu.make_async_copy(ref, ref, sem).wait()


def part(ref, slot, rows):
    return ref.at[pl.ds(slot * rows, rows)]


def place():
    here = lax.axis_index("dp")
    rank = here % LEVEL
    return here, rank // 2, rank % 2


def put_stats(scores, stat_ref, offset):
    peak = jnp.max(scores, axis=0, keepdims=True)
    total = jnp.sum(jnp.exp(scores - peak), axis=0, keepdims=True)
    stat_ref[pl.ds(offset, 1), :] = peak
    stat_ref[pl.ds(WINDOW + offset, 1), :] = total


def row_stats(scores):
    peak = jnp.max(jnp.max(scores, axis=0), axis=1, keepdims=True)
    total = jnp.sum(jnp.sum(jnp.exp(scores - peak[None]), axis=0), axis=1, keepdims=True)
    return peak, total


def merge(peak_a, total_a, peak_b, total_b):
    peak = jnp.maximum(peak_a, peak_b)
    return peak, total_a * jnp.exp(peak_a - peak) + total_b * jnp.exp(peak_b - peak)


def near_scores(image, sibling, text, t1, t1_y, *refs):
    rows_ref, stat_ref, held, own_ref, sib_ref, sems = refs
    rows = image.shape[0]
    _, q, c = place()
    loads = Loads(sems)
    blocks = [part(held, slot, rows) for slot in range(5)]
    arrived(
        *[
            loads.load(block, (None, ref))
            for block, ref in zip(blocks, (image, sibling, text, t1, t1_y))
        ]
    )
    own, sib, *texts = blocks
    offsets = (0, 4, 6 - 4 * q)
    sib_offsets = (3 + 2 * c, 5 - 4 * q + 2 * c)
    stat_ref[...] = jnp.zeros_like(stat_ref)
    for slot, block in enumerate(texts):
        own_ref[slot] = scores_of(own[...], block[...])
        if slot > 0:
            sib_ref[slot - 1] = scores_of(sib[...], block[...])
    for slot in range(3):
        put_stats(own_ref[slot], stat_ref, offsets[slot])
    for slot in range(2):
        put_stats(sib_ref[slot], stat_ref, sib_offsets[slot])
    lane = lax.broadcasted_iota(jnp.int32, rows_ref.shape, 1)
    columns = (*row_stats(own_ref[...]), *row_stats(sib_ref[...]))
    packed = jnp.zeros(rows_ref.shape, jnp.float32)
    for index, column in enumerate(columns):
        packed = jnp.where(lane == index, column, packed)
    rows_ref[...] = packed


def far_scores(near_rows, near_stat, image, sibling, text, t2_lo, t2_hi, own_y, t2_y, *refs):
    message_ref, held, own_ref, sib_ref, stat_ref, sems = refs
    rows = image.shape[0]
    _, q, c = place()
    loads = Loads(sems)
    own, sib, block, last = [part(held, slot, rows) for slot in range(4)]
    arrived(
        loads.load(own, (None, image)),
        loads.load(block, (q == 0, own_y), (q == 1, t2_y)),
        loads.load(sib, (None, sibling)),
        loads.load(last, *last_cases(q, c == 0, t2_lo, t2_hi, text)),
    )
    stat_ref[...] = near_stat[...]
    offset = 2 + 4 * q
    own_ref[0] = scores_of(own[...], block[...])
    sib_ref[0] = scores_of(sib[...], block[...])
    sib_ref[1] = scores_of(sib[...], last[...])
    put_stats(own_ref[0], stat_ref, offset)
    put_stats(sib_ref[0], stat_ref, offset + 2 * c - 1)
    put_stats(sib_ref[1], stat_ref, 7 - 6 * c)
    columns = [near_rows[:, index:index + 1] for index in range(4)]
    own_rows = merge(*columns[:2], *row_stats(own_ref[...]))
    sib_rows = merge(*columns[2:], *row_stats(sib_ref[...]))
    for index, column in enumerate((*own_rows, *sib_rows)):
        stat_ref[pl.ds(ROW_PLACE + index, 1), :] = as_row(column)
    for index in range(message_ref.shape[0]):
        message_ref[index] = stat_ref[...]


def last_cases(q, moved, low_block, high_block, own):
    return (
        (jnp.logical_and(moved, q == 0), low_block),
        (jnp.logical_and(moved, q == 1), high_block),
        (jnp.logical_not(moved), own),
    )


def sibling_of(index):
    return index + 1 - 2 * (index % 2)


def column_norm(table, text):
    count = table.shape[0]
    text = text % count
    peaks = []
    totals = []
    for offset in range(WINDOW):
        source = (text - offset + count) % count
        if offset % 2:
            source = sibling_of(source)
        peaks.append(table[source, pl.ds(offset, 1), :])
        totals.append(table[source, pl.ds(WINDOW + offset, 1), :])
    peaks = jnp.concatenate(peaks, axis=0)
    totals = jnp.concatenate(totals, axis=0)
    peak = jnp.max(peaks, axis=0, keepdims=True)
    total = jnp.sum(totals * jnp.exp(peaks - peak), axis=0, keepdims=True)
    return peak + jnp.log(total)


def row_norms(table, images):
    count = table.shape[0]
    images = [(image + count) % count for image in images]

    def rows_of(sources, place):
        return jnp.concatenate([table[s, pl.ds(place, 1), :] for s in sources], axis=0)

    others = [sibling_of(image) for image in images]
    peak, total = merge(
        rows_of(images, ROW_PLACE),
        rows_of(images, ROW_PLACE + 1),
        rows_of(others, ROW_PLACE + 2),
        rows_of(others, ROW_PLACE + 3),
    )
    return peak + jnp.log(total)


def mixed(scores, self_norm, other_norm, positive=None):
    combined = jnp.exp(scores - self_norm) + jnp.exp(scores - other_norm)
    if positive is not None:
        combined = combined - 2.0 * positive.astype(jnp.float32)
    return combined.astype(jnp.bfloat16)


def wide_products(loads, mixing, blocks, out_ref, out):
    width = blocks.shape[1]
    step = 256 if width % 256 == 0 else width
    stores = []
    for start in range(0, width, step):
        cols = slice(start, start + step)
        product = jnp.dot(mixing[...], blocks[:, cols], preferred_element_type=jnp.float32)
        out_ref[:, cols] = (half_scale * product).astype(out_ref.dtype)
        stores.append(loads.store(out_ref.at[:, cols], out.at[:, cols]))
    return stores


def tile_products(loads, own, sib, blocks, norms, others, positive, mixes, out_refs, outs):
    rows = own.shape[0]
    for slot in range(4):
        block = part(blocks, slot, rows)
        mixes[0][:, slot * rows:(slot + 1) * rows] = mixed(
            scores_of(own[...], block[...]), norms[0], others[slot],
            positive if slot == 0 else None,
        )
    stores = wide_products(
        loads, mixes[0], blocks.at[pl.ds(0, 4 * rows)], out_refs[0], outs[0]
    )
    for slot in range(1, 5):
        block = part(blocks, slot, rows)
        mixes[1][:, (slot - 1) * rows:slot * rows] = mixed(
            scores_of(sib[...], block[...]), norms[1], others[slot]
        )
    stores += wide_products(
        loads, mixes[1], blocks.at[pl.ds(rows, 4 * rows)], out_refs[1], outs[1]
    )
    for store in stores:
        store.wait()


def image_products(label_ref, table_in, image, sibling, *refs):
    text, t1, t1_y, t2_lo, t2_hi, own_y, t2_y = refs[:7]
    outs, (held, blocks, table, *more) = refs[7:9], refs[9:]
    mixes, out_refs, sems = more[:2], more[2:4], more[4]
    rows = image.shape[0]
    here, q, c = place()
    loads = Loads(sems)
    own, sib = part(held, 0, rows), part(held, 1, rows)
    cases = (
        ((None, text),),
        ((None, t1),),
        ((None, t1_y),),
        ((q == 0, own_y), (q == 1, t2_y)),
        last_cases(q, c == 0, t2_lo, t2_hi, text),
    )
    arrived(
        loads.load(table, (None, table_in)),
        loads.load(own, (None, image)),
        loads.load(sib, (None, sibling)),
        *[loads.load(part(blocks, slot, rows), *case) for slot, case in enumerate(cases)],
    )
    sib_place = sibling_of(here)
    norms = row_norms(table, [here, sib_place])
    norms = [as_column(norms[:1]), as_column(norms[1:])]
    offsets = (0, 4, 6 - 4 * q, 2 + 4 * q, 8 - 8 * c)
    others = [column_norm(table, here + offset) for offset in offsets]
    lane = lax.broadcasted_iota(jnp.int32, (rows, rows), 1)
    match = as_column(label_ref[...].astype(jnp.float32)).astype(jnp.int32)
    positive = match == here * rows + lane
    tile_products(loads, own, sib, blocks, norms, others, positive, mixes, out_refs, outs)


def text_products(label_ref, table_in, text, sibling, *refs):
    image, i1_lo, i1_hi, middle, last, i2_lo, i2_hi, own_y = refs[:8]
    outs, (held, blocks, table, *more) = refs[8:10], refs[10:]
    mixes, out_refs, sems = more[:2], more[2:4], more[4]
    rows = text.shape[0]
    here, q, c = place()
    loads = Loads(sems)
    own, sib = part(held, 0, rows), part(held, 1, rows)
    cases = (
        ((None, image),),
        ((q == 0, i1_lo), (q == 1, i1_hi)),
        ((q == 0, middle), (q == 1, last)),
        ((q == 0, last), (q == 1, own_y)),
        last_cases(q, c == 1, i2_lo, i2_hi, image),
    )
    arrived(
        loads.load(table, (None, table_in)),
        loads.load(own, (None, text)),
        loads.load(sib, (None, sibling)),
        *[loads.load(part(blocks, slot, rows), *case) for slot, case in enumerate(cases)],
    )
    norms = [as_column(column_norm(table, index)) for index in (here, sibling_of(here))]
    offsets = (0, 4, 2 + 4 * q, 6 - 4 * q, 8 * c)
    others = row_norms(table, [here - offset for offset in offsets])
    others = [others[slot:slot + 1] for slot in range(5)]
    sublane = lax.broadcasted_iota(jnp.int32, (rows, rows), 0)
    positive = label_ref[...] == here * rows + sublane
    tile_products(loads, own, sib, blocks, norms, others, positive, mixes, out_refs, outs)


def kernel_call(body, outs, scratch, copies, whole, blocks):
    spaces = [pltpu.VMEM] * len(whole) + [pl.ANY] * len(blocks)
    return pl.pallas_call(
        body,
        out_shape=[out for _, out in outs],
        in_specs=[pl.BlockSpec(memory_space=space) for space in spaces],
        out_specs=[pl.BlockSpec(memory_space=space) for space, _ in outs],
        scratch_shapes=[*scratch, pltpu.SemaphoreType.DMA((copies,))],
        compiler_params=pltpu.CompilerParams(vmem_limit_bytes=vmem_bytes),
        cost_estimate=pl.CostEstimate(
            flops=1000000, bytes_accessed=100000, transcendentals=1000
        ),
        name=body.__name__,
    )(*whole, *blocks)


cores = [(0, 1), (1, 0), (2, 3), (3, 2)]
across = [(0, 2), (1, 3), (2, 0), (3, 1)]


def shards(image, text, labels):
    rows, width = image.shape
    count = lax.axis_size("dp")
    f32 = jnp.float32
    low = (lax.axis_index("dp") % LEVEL) < 2

    def struct(*shape):
        return jax.ShapeDtypeStruct(shape, f32)

    def square(blocks):
        return pltpu.VMEM((blocks, rows, rows), f32)

    def wide(blocks, dtype=jnp.bfloat16):
        return pltpu.VMEM((blocks * rows, width), dtype)

    t1 = send(text, [(r + 4, r) for r in range(4)])
    own_y = send(jnp.where(low, image, text), across)
    image_c = send(image, cores)
    text_c = send(text, cores)
    t2_lo = send(t1, [(4, 0), (5, 1)])
    t2_hi = send(t1, [(6, 2)])
    t1_y = send(after(t1, own_y), across)
    i1_hi = send(after(image, t1), [(-2, 2), (-1, 3)])
    i1_lo = send(after(image, t2_lo), [(-4, 0), (-3, 1)])
    ready = lax.optimization_barrier((t2_lo, i1_hi, t1_y))
    middle = send(jnp.where(low, ready[0], ready[1]), across)

    near_rows, near_stat = kernel_call(
        near_scores,
        [(pltpu.VMEM, struct(rows, 128)), (pltpu.VMEM, struct(TABLE_ROWS, rows))],
        [wide(5), square(3), square(2)], 5, [], [image, image_c, text, t1, t1_y],
    )
    (message,) = kernel_call(
        far_scores, [(pltpu.VMEM, struct(count, TABLE_ROWS, rows))],
        [wide(4), square(1), square(2), pltpu.VMEM((TABLE_ROWS, rows), f32)], 4,
        [near_rows, near_stat], [image, image_c, text, t2_lo, t2_hi, own_y, middle],
    )
    i2_hi = send(i1_hi, [(-2, 2), (-1, 3)])
    i2_lo = send(after(i1_lo, near_stat), [(-3, 1)])
    last = send(jnp.where(low, i1_lo, i2_hi), across)
    table = lax.all_to_all(after(message, i2_lo, i2_hi), "dp", 0, 0, tiled=True)

    def tile_call(body, whole, blocks):
        mix = pltpu.VMEM((rows, 4 * rows), jnp.bfloat16)
        return kernel_call(
            body, [(pl.ANY, struct(rows, width))] * 2,
            [wide(2), wide(5), pltpu.VMEM((count, TABLE_ROWS, rows), f32), mix, mix,
             wide(1, f32), wide(1, f32)], 24, whole, blocks,
        )

    label_row = labels[None, :]
    own_image, sib_image = tile_call(
        image_products, [label_row],
        [table, image, image_c, text, t1, t1_y, t2_lo, t2_hi, own_y, middle],
    )
    own_text, sib_text = tile_call(
        text_products, [label_row],
        [after(table, own_image), text, text_c, image, i1_lo, i1_hi, middle, last, i2_lo, i2_hi,
         own_y],
    )
    return own_image + send(sib_image, cores), own_text + send(sib_text, cores)


def solution(mesh):
    return jax.shard_map(
        shards,
        mesh=mesh,
        in_specs=(P(("groups", "dp"), None), P(("groups", "dp"), None), P(("groups", "dp"))),
        out_specs=(P(("groups", "dp"), None), P(("groups", "dp"), None)),
        check_vma=False,
    )
```

```python
import jax
import jax.numpy as jnp
from jax import lax
from jax.experimental import pallas as pl
from jax.experimental.pallas import tpu as pltpu
from jax.sharding import PartitionSpec as P

WINDOW = 8
LEVEL = 4
ROW_PLACE = 16
TABLE_ROWS = 24

logit_scale = 100.0
half_scale = 50.0
vmem_bytes = 52 * 1024 * 1024


def send(block, moves):
    count = lax.axis_size("dp")
    route = [
        ((level * LEVEL + a) % count, (level * LEVEL + b) % count)
        for level in range(count // LEVEL)
        for a, b in moves
    ]
    return lax.ppermute(block, "dp", route)


def after(block, *earlier):
    return lax.optimization_barrier((block, *earlier))[0]


def scores_of(rows, cols):
    products = lax.dot_general(
        rows, cols, (((1,), (1,)), ((), ())), preferred_element_type=jnp.float32
    )
    return logit_scale * products


def as_column(row):
    return jnp.transpose(jnp.broadcast_to(row, (128, row.shape[1])))[:, :1]


def as_row(column):
    return jnp.transpose(jnp.broadcast_to(column, (column.shape[0], 128)))[:1, :]


class Loads:
    def __init__(self, sems):
        self.sems = sems
        self.used = 0

    def slot(self, ref):
        self.used += 1
        return ref, self.sems.at[self.used - 1]

    def load(self, dest, *cases):
        slot = self.slot(dest)
        for chosen, ref in cases:
            copy = pltpu.make_async_copy(ref, *slot)
            if chosen is None:
                copy.start()
            else:
                pl.when(chosen)(copy.start)
        return slot

    def store(self, source, dest):
        copy = pltpu.make_async_copy(source, *self.slot(dest))
        copy.start()
        return copy


def arrived(*slots):
    for ref, sem in slots:
        pltpu.make_async_copy(ref, ref, sem).wait()


def part(ref, slot, rows):
    return ref.at[pl.ds(slot * rows, rows)]


def place():
    here = lax.axis_index("dp")
    rank = here % LEVEL
    return here, rank // 2, rank % 2


def put_stats(scores, stat_ref, offset):
    peak = jnp.max(scores, axis=0, keepdims=True)
    total = jnp.sum(jnp.exp(scores - peak), axis=0, keepdims=True)
    stat_ref[pl.ds(offset, 1), :] = peak
    stat_ref[pl.ds(WINDOW + offset, 1), :] = total


def row_stats(scores):
    peak = jnp.max(jnp.max(scores, axis=0), axis=1, keepdims=True)
    total = jnp.sum(jnp.sum(jnp.exp(scores - peak[None]), axis=0), axis=1, keepdims=True)
    return peak, total


def merge(peak_a, total_a, peak_b, total_b):
    peak = jnp.maximum(peak_a, peak_b)
    return peak, total_a * jnp.exp(peak_a - peak) + total_b * jnp.exp(peak_b - peak)


def near_scores(image, sibling, text, t1, t1_y, *refs):
    rows_ref, stat_ref, held, own_ref, sib_ref, sems = refs
    rows = image.shape[0]
    _, q, c = place()
    loads = Loads(sems)
    blocks = [part(held, slot, rows) for slot in range(5)]
    arrived(
        *[
            loads.load(block, (None, ref))
            for block, ref in zip(blocks, (image, sibling, text, t1, t1_y))
        ]
    )
    own, sib, *texts = blocks
    offsets = (0, 4, 6 - 4 * q)
    sib_offsets = (3 + 2 * c, 5 - 4 * q + 2 * c)
    stat_ref[...] = jnp.zeros_like(stat_ref)
    for slot, block in enumerate(texts):
        own_ref[slot] = scores_of(own[...], block[...])
        if slot > 0:
            sib_ref[slot - 1] = scores_of(sib[...], block[...])
    for slot in range(3):
        put_stats(own_ref[slot], stat_ref, offsets[slot])
    for slot in range(2):
        put_stats(sib_ref[slot], stat_ref, sib_offsets[slot])
    lane = lax.broadcasted_iota(jnp.int32, rows_ref.shape, 1)
    columns = (*row_stats(own_ref[...]), *row_stats(sib_ref[...]))
    packed = jnp.zeros(rows_ref.shape, jnp.float32)
    for index, column in enumerate(columns):
        packed = jnp.where(lane == index, column, packed)
    rows_ref[...] = packed


def far_scores(near_rows, near_stat, image, sibling, text, t2_lo, t2_hi, own_y, t2_y, *refs):
    message_ref, held, own_ref, sib_ref, stat_ref, sems = refs
    rows = image.shape[0]
    _, q, c = place()
    loads = Loads(sems)
    own, sib, block, last = [part(held, slot, rows) for slot in range(4)]
    arrived(
        loads.load(own, (None, image)),
        loads.load(block, (q == 0, own_y), (q == 1, t2_y)),
        loads.load(sib, (None, sibling)),
        loads.load(last, *last_cases(q, c == 0, t2_lo, t2_hi, text)),
    )
    stat_ref[...] = near_stat[...]
    offset = 2 + 4 * q
    own_ref[0] = scores_of(own[...], block[...])
    sib_ref[0] = scores_of(sib[...], block[...])
    sib_ref[1] = scores_of(sib[...], last[...])
    put_stats(own_ref[0], stat_ref, offset)
    put_stats(sib_ref[0], stat_ref, offset + 2 * c - 1)
    put_stats(sib_ref[1], stat_ref, 7 - 6 * c)
    columns = [near_rows[:, index:index + 1] for index in range(4)]
    own_rows = merge(*columns[:2], *row_stats(own_ref[...]))
    sib_rows = merge(*columns[2:], *row_stats(sib_ref[...]))
    for index, column in enumerate((*own_rows, *sib_rows)):
        stat_ref[pl.ds(ROW_PLACE + index, 1), :] = as_row(column)
    for index in range(message_ref.shape[0]):
        message_ref[index] = stat_ref[...]


def last_cases(q, moved, low_block, high_block, own):
    return (
        (jnp.logical_and(moved, q == 0), low_block),
        (jnp.logical_and(moved, q == 1), high_block),
        (jnp.logical_not(moved), own),
    )


def sibling_of(index):
    return index + 1 - 2 * (index % 2)


def column_norm(table, text):
    count = table.shape[0]
    text = text % count
    peaks = []
    totals = []
    for offset in range(WINDOW):
        source = (text - offset + count) % count
        if offset % 2:
            source = sibling_of(source)
        peaks.append(table[source, pl.ds(offset, 1), :])
        totals.append(table[source, pl.ds(WINDOW + offset, 1), :])
    peaks = jnp.concatenate(peaks, axis=0)
    totals = jnp.concatenate(totals, axis=0)
    peak = jnp.max(peaks, axis=0, keepdims=True)
    total = jnp.sum(totals * jnp.exp(peaks - peak), axis=0, keepdims=True)
    return peak + jnp.log(total)


def row_norms(table, images):
    count = table.shape[0]
    images = [(image + count) % count for image in images]

    def rows_of(sources, place):
        return jnp.concatenate([table[s, pl.ds(place, 1), :] for s in sources], axis=0)

    others = [sibling_of(image) for image in images]
    peak, total = merge(
        rows_of(images, ROW_PLACE),
        rows_of(images, ROW_PLACE + 1),
        rows_of(others, ROW_PLACE + 2),
        rows_of(others, ROW_PLACE + 3),
    )
    return peak + jnp.log(total)


def mixed(scores, self_norm, other_norm, positive=None):
    combined = jnp.exp(scores - self_norm) + jnp.exp(scores - other_norm)
    if positive is not None:
        combined = combined - 2.0 * positive.astype(jnp.float32)
    return combined.astype(jnp.bfloat16)


def wide_products(loads, mixing, blocks, out_ref, out):
    width = blocks.shape[1]
    step = 256 if width % 256 == 0 else width
    stores = []
    for start in range(0, width, step):
        cols = slice(start, start + step)
        product = jnp.dot(mixing[...], blocks[:, cols], preferred_element_type=jnp.float32)
        out_ref[:, cols] = (half_scale * product).astype(out_ref.dtype)
        stores.append(loads.store(out_ref.at[:, cols], out.at[:, cols]))
    return stores


def tile_products(loads, own, sib, blocks, norms, others, positive, mixes, out_refs, outs, late):
    rows = own.shape[0]
    for slot in range(4):
        block = part(blocks, slot, rows)
        mixes[0][:, slot * rows:(slot + 1) * rows] = mixed(
            scores_of(own[...], block[...]), norms[0], others[slot],
            positive if slot == 0 else None,
        )
    stores = wide_products(
        loads, mixes[0], blocks.at[pl.ds(0, 4 * rows)], out_refs[0], outs[0]
    )
    arrived(*late)
    for slot in range(1, 5):
        block = part(blocks, slot, rows)
        mixes[1][:, (slot - 1) * rows:slot * rows] = mixed(
            scores_of(sib[...], block[...]), norms[1], others[slot]
        )
    stores += wide_products(
        loads, mixes[1], blocks.at[pl.ds(rows, 4 * rows)], out_refs[1], outs[1]
    )
    for store in stores:
        store.wait()


def image_products(label_ref, table_in, image, sibling, *refs):
    text, t1, t1_y, t2_lo, t2_hi, own_y, t2_y = refs[:7]
    outs, (held, blocks, table, *more) = refs[7:9], refs[9:]
    mixes, out_refs, sems = more[:2], more[2:4], more[4]
    rows = image.shape[0]
    here, q, c = place()
    loads = Loads(sems)
    own, sib = part(held, 0, rows), part(held, 1, rows)
    cases = (
        ((None, text),),
        ((None, t1),),
        ((None, t1_y),),
        ((q == 0, own_y), (q == 1, t2_y)),
        last_cases(q, c == 0, t2_lo, t2_hi, text),
    )
    arrived(
        loads.load(table, (None, table_in)),
        loads.load(own, (None, image)),
        *[loads.load(part(blocks, slot, rows), *cases[slot]) for slot in range(4)],
    )
    late = [loads.load(sib, (None, sibling)), loads.load(part(blocks, 4, rows), *cases[4])]
    sib_place = sibling_of(here)
    norms = row_norms(table, [here, sib_place])
    norms = [as_column(norms[:1]), as_column(norms[1:])]
    offsets = (0, 4, 6 - 4 * q, 2 + 4 * q, 8 - 8 * c)
    others = [column_norm(table, here + offset) for offset in offsets]
    lane = lax.broadcasted_iota(jnp.int32, (rows, rows), 1)
    match = as_column(label_ref[...].astype(jnp.float32)).astype(jnp.int32)
    positive = match == here * rows + lane
    tile_products(loads, own, sib, blocks, norms, others, positive, mixes, out_refs, outs, late)


def text_products(label_ref, table_in, text, sibling, *refs):
    image, i1_lo, i1_hi, middle, last, i2_lo, i2_hi, own_y = refs[:8]
    outs, (held, blocks, table, *more) = refs[8:10], refs[10:]
    mixes, out_refs, sems = more[:2], more[2:4], more[4]
    rows = text.shape[0]
    here, q, c = place()
    loads = Loads(sems)
    own, sib = part(held, 0, rows), part(held, 1, rows)
    cases = (
        ((None, image),),
        ((q == 0, i1_lo), (q == 1, i1_hi)),
        ((q == 0, middle), (q == 1, last)),
        ((q == 0, last), (q == 1, own_y)),
        last_cases(q, c == 1, i2_lo, i2_hi, image),
    )
    arrived(
        loads.load(table, (None, table_in)),
        loads.load(own, (None, text)),
        *[loads.load(part(blocks, slot, rows), *cases[slot]) for slot in range(4)],
    )
    late = [loads.load(sib, (None, sibling)), loads.load(part(blocks, 4, rows), *cases[4])]
    norms = [as_column(column_norm(table, index)) for index in (here, sibling_of(here))]
    offsets = (0, 4, 2 + 4 * q, 6 - 4 * q, 8 * c)
    others = row_norms(table, [here - offset for offset in offsets])
    others = [others[slot:slot + 1] for slot in range(5)]
    sublane = lax.broadcasted_iota(jnp.int32, (rows, rows), 0)
    positive = label_ref[...] == here * rows + sublane
    tile_products(loads, own, sib, blocks, norms, others, positive, mixes, out_refs, outs, late)


def kernel_call(body, outs, scratch, copies, whole, blocks):
    spaces = [pltpu.VMEM] * len(whole) + [pl.ANY] * len(blocks)
    return pl.pallas_call(
        body,
        out_shape=[out for _, out in outs],
        in_specs=[pl.BlockSpec(memory_space=space) for space in spaces],
        out_specs=[pl.BlockSpec(memory_space=space) for space, _ in outs],
        scratch_shapes=[*scratch, pltpu.SemaphoreType.DMA((copies,))],
        compiler_params=pltpu.CompilerParams(vmem_limit_bytes=vmem_bytes),
        cost_estimate=pl.CostEstimate(
            flops=1000000, bytes_accessed=100000, transcendentals=1000
        ),
        name=body.__name__,
    )(*whole, *blocks)


cores = [(0, 1), (1, 0), (2, 3), (3, 2)]
across = [(0, 2), (1, 3), (2, 0), (3, 1)]


def shards(image, text, labels):
    rows, width = image.shape
    count = lax.axis_size("dp")
    f32 = jnp.float32
    low = (lax.axis_index("dp") % LEVEL) < 2

    def struct(*shape):
        return jax.ShapeDtypeStruct(shape, f32)

    def square(blocks):
        return pltpu.VMEM((blocks, rows, rows), f32)

    def wide(blocks, dtype=jnp.bfloat16):
        return pltpu.VMEM((blocks * rows, width), dtype)

    t1 = send(text, [(r + 4, r) for r in range(4)])
    own_y = send(jnp.where(low, image, text), across)
    image_c = send(image, cores)
    text_c = send(text, cores)
    t2_lo = send(t1, [(4, 0), (5, 1)])
    t2_hi = send(t1, [(6, 2)])
    t1_y = send(after(t1, own_y), across)
    i1_hi = send(after(image, t1), [(-2, 2), (-1, 3)])
    i1_lo = send(after(image, t2_lo), [(-4, 0), (-3, 1)])
    ready = lax.optimization_barrier((t2_lo, i1_hi, t1_y))
    middle = send(jnp.where(low, ready[0], ready[1]), across)

    near_rows, near_stat = kernel_call(
        near_scores,
        [(pltpu.VMEM, struct(rows, 128)), (pltpu.VMEM, struct(TABLE_ROWS, rows))],
        [wide(5), square(3), square(2)], 5, [], [image, image_c, text, t1, t1_y],
    )
    (message,) = kernel_call(
        far_scores, [(pltpu.VMEM, struct(count, TABLE_ROWS, rows))],
        [wide(4), square(1), square(2), pltpu.VMEM((TABLE_ROWS, rows), f32)], 4,
        [near_rows, near_stat], [image, image_c, text, t2_lo, t2_hi, own_y, middle],
    )
    i2_hi = send(i1_hi, [(-2, 2), (-1, 3)])
    i2_lo = send(after(i1_lo, near_stat), [(-3, 1)])
    last = send(jnp.where(low, i1_lo, i2_hi), across)
    table = lax.all_to_all(after(message, i2_lo, i2_hi), "dp", 0, 0, tiled=True)

    def tile_call(body, whole, blocks):
        mix = pltpu.VMEM((rows, 4 * rows), jnp.bfloat16)
        return kernel_call(
            body, [(pl.ANY, struct(rows, width))] * 2,
            [wide(2), wide(5), pltpu.VMEM((count, TABLE_ROWS, rows), f32), mix, mix,
             wide(1, f32), wide(1, f32)], 24, whole, blocks,
        )

    label_row = labels[None, :]
    own_image, sib_image = tile_call(
        image_products, [label_row],
        [table, image, image_c, text, t1, t1_y, t2_lo, t2_hi, own_y, middle],
    )
    own_text, sib_text = tile_call(
        text_products, [label_row],
        [after(table, own_image), text, text_c, image, i1_lo, i1_hi, middle, last, i2_lo, i2_hi,
         own_y],
    )
    return own_image + send(sib_image, cores), own_text + send(sib_text, cores)


def solution(mesh):
    return jax.shard_map(
        shards,
        mesh=mesh,
        in_specs=(P(("groups", "dp"), None), P(("groups", "dp"), None), P(("groups", "dp"))),
        out_specs=(P(("groups", "dp"), None), P(("groups", "dp"), None)),
        check_vma=False,
    )
```

```python
import jax
import jax.numpy as jnp
from jax import lax
from jax.experimental import pallas as pl
from jax.experimental.pallas import tpu as pltpu
from jax.sharding import PartitionSpec as P

WINDOW = 8
LEVEL = 4
ROW_PLACE = 16
TABLE_ROWS = 24

logit_scale = 100.0
half_scale = 50.0
vmem_bytes = 52 * 1024 * 1024


def send(block, moves):
    count = lax.axis_size("dp")
    route = [
        ((level * LEVEL + a) % count, (level * LEVEL + b) % count)
        for level in range(count // LEVEL)
        for a, b in moves
    ]
    return lax.ppermute(block, "dp", route)


def after(block, *earlier):
    return lax.optimization_barrier((block, *earlier))[0]


def scores_of(rows, cols):
    products = lax.dot_general(
        rows, cols, (((1,), (1,)), ((), ())), preferred_element_type=jnp.float32
    )
    return logit_scale * products


def as_column(row):
    return jnp.transpose(jnp.broadcast_to(row, (128, row.shape[1])))[:, :1]


def as_row(column):
    return jnp.transpose(jnp.broadcast_to(column, (column.shape[0], 128)))[:1, :]


class Loads:
    def __init__(self, sems):
        self.sems = sems
        self.used = 0

    def slot(self, ref):
        self.used += 1
        return ref, self.sems.at[self.used - 1]

    def load(self, dest, *cases):
        slot = self.slot(dest)
        for chosen, ref in cases:
            copy = pltpu.make_async_copy(ref, *slot)
            if chosen is None:
                copy.start()
            else:
                pl.when(chosen)(copy.start)
        return slot

    def store(self, source, dest):
        copy = pltpu.make_async_copy(source, *self.slot(dest))
        copy.start()
        return copy


def arrived(*slots):
    for ref, sem in slots:
        pltpu.make_async_copy(ref, ref, sem).wait()


def part(ref, slot, rows):
    return ref.at[pl.ds(slot * rows, rows)]


def place():
    here = lax.axis_index("dp")
    rank = here % LEVEL
    return here, rank // 2, rank % 2


def put_stats(scores, stat_ref, offset):
    peak = jnp.max(scores, axis=0, keepdims=True)
    total = jnp.sum(jnp.exp(scores - peak), axis=0, keepdims=True)
    stat_ref[pl.ds(offset, 1), :] = peak
    stat_ref[pl.ds(WINDOW + offset, 1), :] = total


def row_stats(scores):
    peak = jnp.max(jnp.max(scores, axis=0), axis=1, keepdims=True)
    total = jnp.sum(jnp.sum(jnp.exp(scores - peak[None]), axis=0), axis=1, keepdims=True)
    return peak, total


def merge(peak_a, total_a, peak_b, total_b):
    peak = jnp.maximum(peak_a, peak_b)
    return peak, total_a * jnp.exp(peak_a - peak) + total_b * jnp.exp(peak_b - peak)


def near_scores(image, sibling, text, t1, t1_y, *refs):
    rows_ref, stat_ref, held, own_ref, sib_ref, sems = refs
    rows = image.shape[0]
    _, q, c = place()
    loads = Loads(sems)
    blocks = [part(held, slot, rows) for slot in range(5)]
    arrived(
        *[
            loads.load(block, (None, ref))
            for block, ref in zip(blocks, (image, sibling, text, t1, t1_y))
        ]
    )
    own, sib, *texts = blocks
    offsets = (0, 4, 6 - 4 * q)
    sib_offsets = (3 + 2 * c, 5 - 4 * q + 2 * c)
    stat_ref[...] = jnp.zeros_like(stat_ref)
    for slot, block in enumerate(texts):
        own_ref[slot] = scores_of(own[...], block[...])
        if slot > 0:
            sib_ref[slot - 1] = scores_of(sib[...], block[...])
    for slot in range(3):
        put_stats(own_ref[slot], stat_ref, offsets[slot])
    for slot in range(2):
        put_stats(sib_ref[slot], stat_ref, sib_offsets[slot])
    lane = lax.broadcasted_iota(jnp.int32, rows_ref.shape, 1)
    columns = (*row_stats(own_ref[...]), *row_stats(sib_ref[...]))
    packed = jnp.zeros(rows_ref.shape, jnp.float32)
    for index, column in enumerate(columns):
        packed = jnp.where(lane == index, column, packed)
    rows_ref[...] = packed


def far_scores(near_rows, near_stat, image, sibling, text, t2_lo, t2_hi, own_y, t2_y, *refs):
    message_ref, held, own_ref, sib_ref, stat_ref, sems = refs
    rows = image.shape[0]
    _, q, c = place()
    loads = Loads(sems)
    own, sib, block, last = [part(held, slot, rows) for slot in range(4)]
    arrived(
        loads.load(own, (None, image)),
        loads.load(block, (q == 0, own_y), (q == 1, t2_y)),
        loads.load(sib, (None, sibling)),
        loads.load(last, *last_cases(q, c == 0, t2_lo, t2_hi, text)),
    )
    stat_ref[...] = near_stat[...]
    offset = 2 + 4 * q
    own_ref[0] = scores_of(own[...], block[...])
    sib_ref[0] = scores_of(sib[...], block[...])
    sib_ref[1] = scores_of(sib[...], last[...])
    put_stats(own_ref[0], stat_ref, offset)
    put_stats(sib_ref[0], stat_ref, offset + 2 * c - 1)
    put_stats(sib_ref[1], stat_ref, 7 - 6 * c)
    columns = [near_rows[:, index:index + 1] for index in range(4)]
    own_rows = merge(*columns[:2], *row_stats(own_ref[...]))
    sib_rows = merge(*columns[2:], *row_stats(sib_ref[...]))
    for index, column in enumerate((*own_rows, *sib_rows)):
        stat_ref[pl.ds(ROW_PLACE + index, 1), :] = as_row(column)
    for index in range(message_ref.shape[0]):
        message_ref[index] = stat_ref[...]


def last_cases(q, moved, low_block, high_block, own):
    return (
        (jnp.logical_and(moved, q == 0), low_block),
        (jnp.logical_and(moved, q == 1), high_block),
        (jnp.logical_not(moved), own),
    )


def sibling_of(index):
    return index + 1 - 2 * (index % 2)


def column_norm(table, text):
    count = table.shape[0]
    text = text % count
    peaks = []
    totals = []
    for offset in range(WINDOW):
        source = (text - offset + count) % count
        if offset % 2:
            source = sibling_of(source)
        peaks.append(table[source, pl.ds(offset, 1), :])
        totals.append(table[source, pl.ds(WINDOW + offset, 1), :])
    peaks = jnp.concatenate(peaks, axis=0)
    totals = jnp.concatenate(totals, axis=0)
    peak = jnp.max(peaks, axis=0, keepdims=True)
    total = jnp.sum(totals * jnp.exp(peaks - peak), axis=0, keepdims=True)
    return peak + jnp.log(total)


def row_norms(table, images):
    count = table.shape[0]
    images = [(image + count) % count for image in images]

    def rows_of(sources, place):
        return jnp.concatenate([table[s, pl.ds(place, 1), :] for s in sources], axis=0)

    others = [sibling_of(image) for image in images]
    peak, total = merge(
        rows_of(images, ROW_PLACE),
        rows_of(images, ROW_PLACE + 1),
        rows_of(others, ROW_PLACE + 2),
        rows_of(others, ROW_PLACE + 3),
    )
    return peak + jnp.log(total)


def mixed(scores, self_norm, other_norm, positive=None):
    combined = jnp.exp(scores - self_norm) + jnp.exp(scores - other_norm)
    if positive is not None:
        combined = combined - 2.0 * positive.astype(jnp.float32)
    return combined.astype(jnp.bfloat16)


def wide_products(loads, mixing, blocks, out_ref, out):
    width = blocks.shape[1]
    step = 256 if width % 256 == 0 else width
    stores = []
    for start in range(0, width, step):
        cols = slice(start, start + step)
        product = jnp.dot(mixing[...], blocks[:, cols], preferred_element_type=jnp.float32)
        out_ref[:, cols] = (half_scale * product).astype(out_ref.dtype)
        stores.append(loads.store(out_ref.at[:, cols], out.at[:, cols]))
    return stores


def tile_products(loads, own, sib, blocks, norms, others, positive, mixes, out_refs, outs, late):
    rows = own.shape[0]
    for slot in range(4):
        block = part(blocks, slot, rows)
        mixes[0][:, slot * rows:(slot + 1) * rows] = mixed(
            scores_of(own[...], block[...]), norms[0], others[slot],
            positive if slot == 0 else None,
        )
    stores = wide_products(
        loads, mixes[0], blocks.at[pl.ds(0, 4 * rows)], out_refs[0], outs[0]
    )
    arrived(*late)
    for slot in range(1, 5):
        block = part(blocks, slot, rows)
        mixes[1][:, (slot - 1) * rows:slot * rows] = mixed(
            scores_of(sib[...], block[...]), norms[1], others[slot]
        )
    stores += wide_products(
        loads, mixes[1], blocks.at[pl.ds(rows, 4 * rows)], out_refs[1], outs[1]
    )
    for store in stores:
        store.wait()


def image_products(label_ref, table_in, image, sibling, *refs):
    text, t1, t1_y, t2_lo, t2_hi, own_y, t2_y = refs[:7]
    outs, (held, blocks, table, *more) = refs[7:9], refs[9:]
    mixes, out_refs, sems = more[:2], more[2:4], more[4]
    rows = image.shape[0]
    here, q, c = place()
    loads = Loads(sems)
    own, sib = part(held, 0, rows), part(held, 1, rows)
    cases = (
        ((None, text),),
        ((None, t1),),
        ((None, t1_y),),
        ((q == 0, own_y), (q == 1, t2_y)),
        last_cases(q, c == 0, t2_lo, t2_hi, text),
    )
    arrived(
        loads.load(table, (None, table_in)),
        loads.load(own, (None, image)),
        *[loads.load(part(blocks, slot, rows), *cases[slot]) for slot in range(4)],
    )
    late = [loads.load(sib, (None, sibling)), loads.load(part(blocks, 4, rows), *cases[4])]
    sib_place = sibling_of(here)
    norms = row_norms(table, [here, sib_place])
    norms = [as_column(norms[:1]), as_column(norms[1:])]
    offsets = (0, 4, 6 - 4 * q, 2 + 4 * q, 8 - 8 * c)
    others = [column_norm(table, here + offset) for offset in offsets]
    lane = lax.broadcasted_iota(jnp.int32, (rows, rows), 1)
    match = as_column(label_ref[...].astype(jnp.float32)).astype(jnp.int32)
    positive = match == here * rows + lane
    tile_products(loads, own, sib, blocks, norms, others, positive, mixes, out_refs, outs, late)


def text_products(label_ref, table_in, text, sibling, *refs):
    image, i1_lo, i1_hi, middle, last, i2_lo, i2_hi, own_y = refs[:8]
    outs, (held, blocks, table, *more) = refs[8:10], refs[10:]
    mixes, out_refs, sems = more[:2], more[2:4], more[4]
    rows = text.shape[0]
    here, q, c = place()
    loads = Loads(sems)
    own, sib = part(held, 0, rows), part(held, 1, rows)
    cases = (
        ((None, image),),
        ((q == 0, i1_lo), (q == 1, i1_hi)),
        ((q == 0, middle), (q == 1, last)),
        ((q == 0, last), (q == 1, own_y)),
        last_cases(q, c == 1, i2_lo, i2_hi, image),
    )
    arrived(
        loads.load(table, (None, table_in)),
        loads.load(own, (None, text)),
        *[loads.load(part(blocks, slot, rows), *cases[slot]) for slot in range(4)],
    )
    late = [loads.load(sib, (None, sibling)), loads.load(part(blocks, 4, rows), *cases[4])]
    norms = [as_column(column_norm(table, index)) for index in (here, sibling_of(here))]
    offsets = (0, 4, 2 + 4 * q, 6 - 4 * q, 8 * c)
    others = row_norms(table, [here - offset for offset in offsets])
    others = [others[slot:slot + 1] for slot in range(5)]
    sublane = lax.broadcasted_iota(jnp.int32, (rows, rows), 0)
    positive = label_ref[...] == here * rows + sublane
    tile_products(loads, own, sib, blocks, norms, others, positive, mixes, out_refs, outs, late)


def kernel_call(body, outs, scratch, copies, whole, blocks):
    products = body in (image_products, text_products)
    vmem_limit = vmem_bytes if products else vmem_bytes // 2
    spaces = [pltpu.VMEM] * len(whole) + [pl.ANY] * len(blocks)
    return pl.pallas_call(
        body,
        out_shape=[out for _, out in outs],
        in_specs=[pl.BlockSpec(memory_space=space) for space in spaces],
        out_specs=[pl.BlockSpec(memory_space=space) for space, _ in outs],
        scratch_shapes=[*scratch, pltpu.SemaphoreType.DMA((copies,))],
        compiler_params=pltpu.CompilerParams(vmem_limit_bytes=vmem_limit),
        cost_estimate=pl.CostEstimate(
            flops=1000000, bytes_accessed=100000, transcendentals=1000
        ),
        name=body.__name__,
    )(*whole, *blocks)


cores = [(0, 1), (1, 0), (2, 3), (3, 2)]
across = [(0, 2), (1, 3), (2, 0), (3, 1)]


def shards(image, text, labels):
    rows, width = image.shape
    count = lax.axis_size("dp")
    f32 = jnp.float32
    low = (lax.axis_index("dp") % LEVEL) < 2

    def struct(*shape):
        return jax.ShapeDtypeStruct(shape, f32)

    def square(blocks):
        return pltpu.VMEM((blocks, rows, rows), f32)

    def wide(blocks, dtype=jnp.bfloat16):
        return pltpu.VMEM((blocks * rows, width), dtype)

    t1 = send(text, [(r + 4, r) for r in range(4)])
    own_y = send(jnp.where(low, image, text), across)
    image_c = send(image, cores)
    text_c = send(text, cores)
    t2_lo = send(t1, [(4, 0), (5, 1)])
    t2_hi = send(t1, [(6, 2)])
    t1_y = send(after(t1, own_y), across)
    i1_hi = send(after(image, t1), [(-2, 2), (-1, 3)])
    i1_lo = send(after(image, t2_lo), [(-4, 0), (-3, 1)])
    ready = lax.optimization_barrier((t2_lo, i1_hi, t1_y))
    middle = send(jnp.where(low, ready[0], ready[1]), across)

    near_rows, near_stat = kernel_call(
        near_scores,
        [(pltpu.VMEM, struct(rows, 128)), (pltpu.VMEM, struct(TABLE_ROWS, rows))],
        [wide(5), square(3), square(2)], 5, [], [image, image_c, text, t1, t1_y],
    )
    (message,) = kernel_call(
        far_scores, [(pltpu.VMEM, struct(count, TABLE_ROWS, rows))],
        [wide(4), square(1), square(2), pltpu.VMEM((TABLE_ROWS, rows), f32)], 4,
        [near_rows, near_stat], [image, image_c, text, t2_lo, t2_hi, own_y, middle],
    )
    i2_hi = send(i1_hi, [(-2, 2), (-1, 3)])
    i2_lo = send(after(i1_lo, near_stat), [(-3, 1)])
    last = send(jnp.where(low, i1_lo, i2_hi), across)
    table = lax.all_to_all(after(message, i2_lo, i2_hi), "dp", 0, 0, tiled=True)

    def tile_call(body, whole, blocks):
        mix = pltpu.VMEM((rows, 4 * rows), jnp.bfloat16)
        return kernel_call(
            body, [(pl.ANY, struct(rows, width))] * 2,
            [wide(2), wide(5), pltpu.VMEM((count, TABLE_ROWS, rows), f32), mix, mix,
             wide(1, f32), wide(1, f32)], 24, whole, blocks,
        )

    label_row = labels[None, :]
    own_image, sib_image = tile_call(
        image_products, [label_row],
        [table, image, image_c, text, t1, t1_y, t2_lo, t2_hi, own_y, middle],
    )
    own_text, sib_text = tile_call(
        text_products, [label_row],
        [after(table, own_image), text, text_c, image, i1_lo, i1_hi, middle, last, i2_lo, i2_hi,
         own_y],
    )
    return own_image + send(sib_image, cores), own_text + send(sib_text, cores)


def solution(mesh):
    return jax.shard_map(
        shards,
        mesh=mesh,
        in_specs=(P(("groups", "dp"), None), P(("groups", "dp"), None), P(("groups", "dp"))),
        out_specs=(P(("groups", "dp"), None), P(("groups", "dp"), None)),
        check_vma=False,
    )
```
